32 devices in a mesh: row: 8 (over y, x, core), col: 4 (over z).
Axes of the slice: x: 2, y: 2, z: 4, core: 2. Of those that a mesh axis runs over, the one named last changes fastest.
Arguments:
- tokens: bfloat16 [3072, 6144], P('row'), may hold values from -6 to 6
- ln_gain: float32 [6144], replicated, may hold values from 0.1 to 1.9
- qkv_weight: bfloat16 [6144, 3, 3072], P('row', None, 'col'), may hold values from -0.078125 to 0.078125
- q_gain: float32 [24, 128], P('col'), may hold values from 0.4 to 5
- k_gain: float32 [24, 128], P('col'), may hold values from 0.4 to 5
- block_mask: int32 [24, 24, 24], P('col'), may hold values from 0 to 1, as said below
- out_weight: bfloat16 [3072, 6144], P('row', 'col'), may hold values from -0.875 to 0.875
- grad_out: bfloat16 [3072, 6144], P('row', 'col'), may hold values from -6 to 6
Outputs:
- branch_out: bfloat16 [3072, 6144], P('row', 'col')
- out_weight_grad: float32 [3072, 6144], P('row', 'col')
The draws below stay inside these ranges and needn't reach their ends.
Inputs may be any that keep to these rules, and one draw needn't show every extreme that they name: `block_mask`: entries are 0 or 1; every block sees itself; spectral heads see their spatial window, spatial heads their band group, some heads both, with further blocks scattered at rates that differ by head and by band.
All inputs are finite; a program needn't handle non-finite values.
Results may differ from the reference program's by a relative error of at most 0.014.
The reference program's roundings to bfloat16 on the way (of `normed`, `weights` and `attn`) count: a program that leaves them out, or rounds other values in their place, can miss the bound.
Values may be sent and summed in bfloat16 or wider, within the bound.
A program may use at most 128 MiB of HBM per device.

```python
import jax
import jax.numpy as jnp
from jax import lax

D = 6144
HS = 128
HEADS = 24
HD = 3072
TOKENS = 3072
BLOCK = 128
BANDS = 8


def draw_block_mask(key, part):
    nblocks = TOKENS // BLOCK
    key_kind, key_rate, key_extra = jax.random.split(key, 3)
    head_kind = jax.random.randint(key_kind, (HEADS,), 0, 3)
    rate_base = jax.random.randint(key_rate, (HEADS,), 1, 6)
    block_ids = jnp.arange(nblocks, dtype=jnp.int32)
    band_id = block_ids % BANDS
    window = block_ids // BANDS
    same_window = (window[:, None] == window[None, :])[None]
    same_band = (band_id[:, None] == band_id[None, :])[None]
    kind_grid = head_kind[:, None, None]
    base_mask = jnp.where(kind_grid == 0, same_window, jnp.where(kind_grid == 1, same_band, same_window | same_band))
    threshold = rate_base[:, None, None] * (1 + band_id[None, :, None] % 4)
    extra = jax.random.randint(key_extra, (HEADS, nblocks, nblocks), 0, 32) < threshold
    diagonal = (block_ids[:, None] == block_ids[None, :])[None]
    return (base_mask | extra | diagonal).astype(jnp.int32)


def gain_draw(key):
    return 1.0 + 0.3 * jnp.clip(jax.random.normal(key, (HEADS, HS), jnp.float32), -2.0, 2.0)


def draw_q_gain(key, part):
    return gain_draw(jax.random.fold_in(key, 11))


def draw_k_gain(key, part):
    return gain_draw(jax.random.fold_in(key, 23))


def level_of(own_key, dims, shards, low, top_value):
    factor_of, own = 1.0, jax.random.fold_in(own_key, 6)
    for axis_at, parts in shards:
        heights = jnp.exp(jax.random.uniform(jax.random.fold_in(own, axis_at), (parts,), jnp.float32, low / len(shards), top_value / len(shards)))
        factor_of = factor_of * jnp.repeat(heights, dims[axis_at] // parts).reshape([-1 if axis == axis_at else 1 for axis in range(len(dims))])
    return factor_of


def scatter_about(stream_key, dims, width, most, pieces=(), kind=jnp.bfloat16):
    result = jax.random.normal(stream_key, dims, jnp.float32) * width
    if len(pieces) > 0:
        result = level_of(stream_key, dims, pieces, -0.22, 0.18) * result
    return jnp.clip(result, min=-most, max=most).astype(kind)


def setup_inputs(seed: int = 0) -> dict:
    seeds = jax.random.split(jax.random.key(seed), 9)
    return {
        "tokens": scatter_about(seeds[0], (TOKENS, D), 1.0, 6.0, ((0, 8),)),
        "ln_gain": jnp.clip(1.0 + 0.18 * jax.random.normal(seeds[1], (D,), jnp.float32), 0.1, 1.9),
        "qkv_weight": scatter_about(seeds[2], (D, 3, HD), D ** -0.5, 0.078125, ((0, 8), (2, 4))),
        "q_gain": draw_q_gain(jax.random.fold_in(seeds[8], 71), 0),
        "k_gain": draw_k_gain(jax.random.fold_in(seeds[8], 71), 0),
        "block_mask": draw_block_mask(jax.random.fold_in(seeds[8], 71), 0),
        "out_weight": scatter_about(seeds[6], (HD, D), (HD // 64) ** -0.5, 0.875, ((0, 8), (1, 4))),
        "grad_out": scatter_about(seeds[7], (TOKENS, D), 1.0, 6.0, ((0, 8), (1, 4))),
    }


EPS = 1e-06

def norm_rows(values, gain):
    center = lax.optimization_barrier(jnp.mean(values, axis=-1, keepdims=True))
    shifted = values - center
    variance = lax.optimization_barrier(jnp.mean(shifted * shifted, axis=-1, keepdims=True))
    return shifted * lax.rsqrt(variance + EPS) * gain

def reference(tokens, ln_gain, qkv_weight, q_gain, k_gain, block_mask, out_weight, grad_out):
    normed = norm_rows(tokens.astype(jnp.float32), ln_gain).astype(jnp.bfloat16)
    flat_weight = qkv_weight.reshape(D, 3 * HD)
    mixed = jnp.dot(normed, flat_weight, preferred_element_type=jnp.float32).reshape(TOKENS, 3, HEADS, HS)
    queries = norm_rows(mixed[:, 0], q_gain).astype(jnp.bfloat16)
    keys_all = norm_rows(mixed[:, 1], k_gain).astype(jnp.bfloat16)
    values_all = mixed[:, 2].astype(jnp.bfloat16)
    nblocks = TOKENS // BLOCK
    score_scale = HS ** (-0.5)

    def one_head(operands):
        query_head, key_head, value_head, mask_head = operands
        scores = jnp.dot(query_head, key_head.T, preferred_element_type=jnp.float32) * score_scale
        scores = scores.reshape(nblocks, BLOCK, nblocks, BLOCK)
        is_live = mask_head[:, None, :, None] > 0
        scores = jnp.where(is_live, scores, -1e+30)
        top_score = lax.optimization_barrier(jnp.max(scores, axis=(2, 3), keepdims=True))
        expo = jnp.where(is_live, jnp.exp(scores - top_score), 0.0)
        denom = lax.optimization_barrier(jnp.sum(expo, axis=(2, 3))).reshape(TOKENS, 1)
        weights = expo.reshape(TOKENS, TOKENS).astype(jnp.bfloat16)
        return (jnp.dot(weights, value_head, preferred_element_type=jnp.float32) / denom).astype(jnp.bfloat16)
    per_head = lax.map(one_head, (queries.transpose(1, 0, 2), keys_all.transpose(1, 0, 2), values_all.transpose(1, 0, 2), block_mask))
    attn = per_head.transpose(1, 0, 2).reshape(TOKENS, HD)
    branch_out = jnp.dot(attn, out_weight, preferred_element_type=jnp.float32).astype(jnp.bfloat16)
    out_weight_grad = jnp.dot(attn.T, grad_out, preferred_element_type=jnp.float32)
    return (branch_out, out_weight_grad)
```

```python
import functools

import jax
import jax.numpy as jnp
from jax import lax
from jax.experimental import pallas as pl
from jax.experimental.pallas import tpu as pltpu
from jax.sharding import PartitionSpec as P

HS = 128
BLOCK = 128
EPS = 1e-06
MESH = pl.DeviceIdType.MESH
SUBS = 2


def norm_rows(values, gain):
    center = jnp.mean(values, axis=-1, keepdims=True)
    shifted = values - center
    variance = jnp.mean(shifted * shifted, axis=-1, keepdims=True)
    return shifted * lax.rsqrt(variance + EPS) * gain


def flip(index, bit):
    return index + bit - 2 * bit * ((index // bit) % 2)


def places():
    row, col = lax.axis_index("row"), lax.axis_index("col")
    return row, col, flip(row, 1), flip(row, 2), flip(row, 4), flip(flip(row, 2), 4)


def remote(src, dst, send, recv, device):
    return pltpu.make_async_remote_copy(
        src_ref=src, dst_ref=dst, send_sem=send, recv_sem=recv, device_id=device, device_id_type=MESH
    )


def project_kernel(ncol, tok_ref, w_ref, qg_ref, kg_ref, out_ref, wbuf, tbuf, acc,
                   w_recv, w_send, t_recv, t_send):
    row, col, mate, xn, yn, dn = places()
    half = (row // 2) % 2
    rows_tok, depth = tok_ref.shape[1], tok_ref.shape[2]
    per = tok_ref.shape[0] // ncol
    width = w_ref.shape[-1]
    tile = width // 3
    sub = depth // SUBS

    barrier = pltpu.get_barrier_semaphore()
    for other in (mate, xn, yn):
        pl.semaphore_signal(barrier, inc=1, device_id=(other, col), device_id_type=MESH)

    @pl.when(col > 0)
    def _():
        pl.semaphore_signal(barrier, inc=1, device_id=(row, col - 1), device_id_type=MESH)

    @pl.when(col < ncol - 1)
    def _():
        pl.semaphore_signal(barrier, inc=1, device_id=(row, col + 1), device_id_type=MESH)

    pl.semaphore_wait(barrier, 3 + jnp.where(col > 0, 1, 0) + jnp.where(col < ncol - 1, 1, 0))

    def wpart(block, s):
        return wbuf.at[block, pl.ds(s * sub, sub)]

    def wown(which, s):
        return w_ref.at[which, pl.ds(s * sub, sub)]

    def wcopy(src, block, s, slot, device):
        return remote(src, wpart(block, s), w_send.at[slot, s], w_recv.at[block, s], (device, col))

    def tcopy(src, block, q, slot, device):
        return remote(src, tbuf.at[block], t_send.at[slot, q], t_recv.at[block], device)

    first = [tcopy(tok_ref.at[col * per + q], col * per + q, q, 0, (xn, col)) for q in range(per)]
    for copy in first:
        copy.start()
    to_y = [wcopy(wown(half, s), row, s, 0, yn) for s in range(SUBS)]
    to_x = [wcopy(wown(1 - half, s), row, s, 1, xn) for s in range(SUBS)]
    to_mate = [wcopy(wown(half, s), row, s, 2, mate) for s in range(SUBS)]
    for copy in to_y + to_mate:
        copy.start()

    own_at = pl.multiple_of(half * rows_tok, rows_tok)
    nbr_at = pl.multiple_of((1 - half) * rows_tok, rows_tok)

    def times(at, left, right, fresh):
        @pl.loop(0, 3)
        def _(t):
            cols = pl.ds(pl.multiple_of(t * tile, tile), tile)
            prod = jnp.dot(left[...], right[:, cols], preferred_element_type=jnp.float32)
            if fresh:
                acc[pl.ds(at, rows_tok), cols] = prod
            else:
                acc[pl.ds(at, rows_tok), cols] += prod

    times(own_at, tok_ref.at[row], w_ref.at[half], True)

    def up(block, q, slot):
        return tcopy(tbuf.at[block], block, q, slot, (row, col + 1))

    def down(block, q, slot):
        return tcopy(tbuf.at[block], block, q, slot, (row, col - 1))

    def t_got(block):
        tcopy(tbuf.at[block], block, 0, 0, (xn, col)).wait_recv()

    def w_got(block, s):
        wcopy(wpart(block, s), block, s, 0, xn).wait_recv()

    def spread(dist, q):
        if dist == 0:
            block = col * per + q
            t_got(block)

            @pl.when(col < ncol - 1)
            def _():
                up(block, q, 1).start()

            @pl.when(col > 0)
            def _():
                down(block, q, 2).start()
            return

        @pl.when(col >= dist)
        def _():
            block = (col - dist) * per + q
            t_got(block)

            @pl.when(col < ncol - 1)
            def _():
                up(block, q, 2 * dist + 1).start()

        @pl.when(col + dist < ncol)
        def _():
            block = (col + dist) * per + q
            t_got(block)

            @pl.when(col > 0)
            def _():
                down(block, q, 2 * dist + 2).start()

    pend = []

    def pass_w(block, s, slots):
        w_got(block, s)
        for slot, device in slots:
            copy = wcopy(wpart(block, s), block, s, slot, device)
            copy.start()
            pend.append(copy)

    for q in range(per):
        spread(0, q)
    for copy in to_x:
        copy.start()
    pass_w(yn, 0, [(3, mate)])
    spread(1, 0)
    pass_w(yn, 1, [(3, mate)])
    spread(1, 1)
    times(own_at, tok_ref.at[yn], wbuf.at[yn], False)
    pass_w(xn, 0, [(4, yn), (5, mate)])
    spread(2, 0)
    pass_w(xn, 1, [(4, yn), (5, mate)])
    spread(2, 1)
    times(own_at, tok_ref.at[xn], wbuf.at[xn], False)
    for block in (mate, flip(mate, 4), flip(mate, 2)):
        for s in range(SUBS):
            w_got(block, s)
        times(own_at, tok_ref.at[block], wbuf.at[block], False)
    for s in range(SUBS):
        pass_w(dn, s, [(6, mate)])
    times(own_at, tok_ref.at[dn], wbuf.at[dn], False)
    for dist in range(3, ncol):
        for q in range(per):
            spread(dist, q)
    times(nbr_at, tbuf.at[row], w_ref.at[half], True)
    for block in (mate, flip(mate, 4), flip(mate, 2), yn, xn, dn):
        times(nbr_at, tbuf.at[block], wbuf.at[block], False)
    last = flip(dn, 1)
    for s in range(SUBS):
        w_got(last, s)
    times(own_at, tok_ref.at[last], wbuf.at[last], False)
    times(nbr_at, tbuf.at[last], wbuf.at[last], False)

    heads = qg_ref.shape[0]
    for kind in range(3):
        for h in range(heads):
            at = (kind * heads + h) * HS
            part = acc[:, at:at + HS]
            if kind < 2:
                part = norm_rows(part, (qg_ref, kg_ref)[kind][h:h + 1, :])
            out_ref[kind, h] = part.astype(jnp.bfloat16)

    for copy in first + to_y + to_x + to_mate + pend:
        copy.wait_send()
    for q in range(per):
        for dist in range(ncol):
            @pl.when((col >= dist) & (col < ncol - 1))
            def _():
                block = (col - dist) * per + q
                up(block, q, 2 * dist + 1).wait_send()

            @pl.when((col + dist < ncol) & (col > 0))
            def _():
                block = (col + dist) * per + q
                down(block, q, 2 * dist + 2).wait_send()


def attend_kernel(qkv_ref, bias_ref, out_ref, kvbuf, recv, send):
    row, col, mate, xn, yn, dn = places()
    heads, rows = qkv_ref.shape[1], qkv_ref.shape[2]
    here = 2 * (row // 4) + row % 2
    yslot = flip(here, 2)
    barrier = pltpu.get_barrier_semaphore()
    for other in (mate, yn):
        pl.semaphore_signal(barrier, inc=1, device_id=(other, col), device_id_type=MESH)
    pl.semaphore_wait(barrier, 2)

    def copy(src, kv, h, slot, way, device):
        return remote(src, kvbuf.at[kv, h, slot], send.at[way, kv, h], recv.at[kv, h, slot], (device, col))

    started = []
    for h in range(heads):
        for kv in range(2):
            for way, device in ((0, yn), (1, mate)):
                one = copy(qkv_ref.at[1 + kv, h], kv, h, here, way, device)
                one.start()
                started.append(one)
            kvbuf[kv, h, here] = qkv_ref[1 + kv, h]
    scale = HS ** (-0.5)
    for h in range(heads):
        for kv in range(2):
            copy(kvbuf.at[kv, h, yslot], kv, h, yslot, 2, mate).wait_recv()
            one = copy(kvbuf.at[kv, h, yslot], kv, h, yslot, 2, mate)
            one.start()
            started.append(one)
    for h in range(heads):
        for kv in range(2):
            copy(kvbuf.at[kv, h, 0], kv, h, flip(here, 1), 2, mate).wait_recv()
            copy(kvbuf.at[kv, h, 0], kv, h, flip(yslot, 1), 2, mate).wait_recv()

        @pl.loop(0, rows // BLOCK)
        def _(b):
            at = pl.ds(pl.multiple_of(b * BLOCK, BLOCK), BLOCK)
            keys = kvbuf[0, h].reshape(4 * rows, HS)
            scores = lax.dot_general(qkv_ref[0, h, at, :], keys, (((1,), (1,)), ((), ())),
                                     preferred_element_type=jnp.float32) * scale
            scores = scores + bias_ref[h, b]
            top = jnp.max(scores, axis=-1, keepdims=True)
            expo = jnp.exp(scores - top)
            denom = jnp.sum(expo, axis=-1, keepdims=True)
            prod = jnp.dot(expo.astype(jnp.bfloat16), kvbuf[1, h].reshape(4 * rows, HS),
                           preferred_element_type=jnp.float32)
            out_ref[at, h * HS:(h + 1) * HS] = (prod / denom).astype(jnp.bfloat16)
    for one in started:
        one.wait_send()


def vmem(count):
    return [pl.BlockSpec(memory_space=pltpu.VMEM)] * count


def attention_fast(ncol, nrow, tokens, ln_gain, qkv_weight, q_gain, k_gain, block_mask):
    tok_rows, feats = tokens.shape
    depth, _, col_width = qkv_weight.shape
    heads = q_gain.shape[0] // 2
    row = lax.axis_index("row")
    half = (row // 2) % 2
    normed = norm_rows(tokens.astype(jnp.float32), ln_gain).astype(jnp.bfloat16)
    normed = normed.reshape(tok_rows, nrow, depth).transpose(1, 0, 2)
    wide = 3 * heads * HS
    weight = qkv_weight.reshape(depth, 3, 2, heads * HS).transpose(2, 0, 1, 3).reshape(2, depth, wide)
    qg = lax.dynamic_slice_in_dim(q_gain, half * heads, heads, 0)
    kg = lax.dynamic_slice_in_dim(k_gain, half * heads, heads, 0)
    dma = pltpu.SemaphoreType.DMA
    qkv = pl.pallas_call(
        functools.partial(project_kernel, ncol),
        out_shape=jax.ShapeDtypeStruct((3, heads, 2 * tok_rows, HS), jnp.bfloat16),
        in_specs=vmem(4),
        out_specs=vmem(1)[0],
        scratch_shapes=[
            pltpu.VMEM((nrow, depth, wide), jnp.bfloat16),
            pltpu.VMEM((nrow, tok_rows, depth), jnp.bfloat16),
            pltpu.VMEM((2 * tok_rows, wide), jnp.float32),
            dma((nrow, SUBS)), dma((7, SUBS)), dma((nrow,)), dma((2 * ncol + 1, nrow // ncol)),
        ],
        compiler_params=pltpu.CompilerParams(
            collective_id=0, has_side_effects=True, vmem_limit_bytes=56 * 2**20),
        name="project",
    )(normed, weight, qg, kg)

    per = tok_rows // BLOCK
    nblocks = block_mask.shape[1]
    mask = lax.dynamic_slice_in_dim(block_mask, half * heads, heads, 0)
    order = mask.reshape(heads, 2, 2, 2, per, 2, 2, 2, per)
    mine = lax.dynamic_index_in_dim(order, row // 4, 1, False)
    mine = lax.dynamic_index_in_dim(mine, row % 2, 2, False)
    mine = mine.transpose(0, 1, 2, 3, 5, 4, 6).reshape(heads, 2 * per, nblocks)
    bias = jnp.where(mine > 0, 0.0, -1e30).astype(jnp.float32)
    bias = jnp.repeat(bias, BLOCK, axis=2).reshape(heads, 2 * per, 1, nblocks * BLOCK)
    return pl.pallas_call(
        attend_kernel,
        out_shape=jax.ShapeDtypeStruct((2 * tok_rows, heads * HS), jnp.bfloat16),
        in_specs=vmem(2),
        out_specs=vmem(1)[0],
        scratch_shapes=[
            pltpu.VMEM((2, heads, 4, 2 * tok_rows, HS), jnp.bfloat16),
            dma((2, heads, 4)), dma((3, 2, heads)),
        ],
        compiler_params=pltpu.CompilerParams(
            collective_id=1, has_side_effects=True, vmem_limit_bytes=48 * 2**20),
        name="attend",
    )(qkv, bias)


def fast_device(ncol, nrow, tokens, ln_gain, qkv_weight, q_gain, k_gain, block_mask, out_weight, grad_out):
    tok_rows = tokens.shape[0]
    row = lax.axis_index("row")
    half = (row // 2) % 2
    attn = attention_fast(ncol, nrow, tokens, ln_gain, qkv_weight, q_gain, k_gain, block_mask)
    out_weight, attn = lax.optimization_barrier((out_weight, attn))
    weight_all = lax.all_gather(out_weight, "row", axis=0, tiled=True)
    own = lax.dynamic_slice_in_dim(attn, half * tok_rows, tok_rows, 0)
    give = lax.dynamic_slice_in_dim(attn, (1 - half) * tok_rows, tok_rows, 0)
    got = lax.ppermute(give, "row", [(i, i ^ 2) for i in range(nrow)])
    first = jnp.where(half == 0, own, got)
    second = jnp.where(half == 0, got, own)
    attn_here = jnp.concatenate([first, second], axis=1)
    whole_attn = lax.all_gather(attn_here, "col", axis=1, tiled=True)
    partial = jnp.einsum("tk,td->kd", whole_attn, grad_out, preferred_element_type=jnp.float32)
    weight_grad = lax.psum_scatter(
        partial.astype(jnp.bfloat16), "row", scatter_dimension=0, tiled=True
    ).astype(jnp.float32)
    branch = jnp.dot(whole_attn, weight_all, preferred_element_type=jnp.float32)
    return branch.astype(jnp.bfloat16), weight_grad


def per_device(tokens, ln_gain, qkv_weight, q_gain, k_gain, block_mask, out_weight, grad_out):
    tok_rows = tokens.shape[0]
    heads_here = q_gain.shape[0]
    col_width = heads_here * HS
    normed = norm_rows(tokens.astype(jnp.float32), ln_gain).astype(jnp.bfloat16)
    portion = lax.all_gather(qkv_weight, "row", axis=0, tiled=True)
    flat_part = portion.reshape(portion.shape[0], 3 * col_width)
    mixed = jnp.dot(normed, flat_part, preferred_element_type=jnp.float32)
    mixed = mixed.reshape(tok_rows, 3, heads_here, HS)
    queries = norm_rows(mixed[:, 0], q_gain).astype(jnp.bfloat16)
    keys_here = norm_rows(mixed[:, 1], k_gain).astype(jnp.bfloat16)
    values_here = mixed[:, 2].astype(jnp.bfloat16)
    nblocks = block_mask.shape[1]
    qblocks = tok_rows // BLOCK
    first_block = lax.axis_index("row") * qblocks
    mask_rows = lax.dynamic_slice_in_dim(block_mask, first_block, qblocks, 1)
    query_blocks = queries.reshape(qblocks, BLOCK, heads_here, HS)
    key_part = lax.all_gather(keys_here, "row", axis=0, tiled=True)
    value_part = lax.all_gather(values_here, "row", axis=0, tiled=True)
    scores = (
        jnp.einsum("abhd,khd->habk", query_blocks, key_part, preferred_element_type=jnp.float32)
        * HS ** (-0.5)
    )
    is_live = jnp.repeat(mask_rows > 0, BLOCK, axis=2)[:, :, None, :]
    scores = jnp.where(is_live, scores, -1e30)
    top = jnp.max(scores, axis=-1, keepdims=True)
    expo = jnp.where(is_live, jnp.exp(scores - top), 0.0)
    denom = jnp.sum(expo, axis=-1)
    accum = jnp.einsum(
        "habk,khd->habd", expo.astype(jnp.bfloat16), value_part, preferred_element_type=jnp.float32
    )
    attn_here = (accum / denom[..., None]).astype(jnp.bfloat16)
    attn_here = attn_here.transpose(1, 2, 0, 3).reshape(tok_rows, col_width)
    whole_attn = lax.all_gather(attn_here, "col", axis=1, tiled=True)
    branch = jnp.dot(
        whole_attn,
        lax.all_gather(out_weight, "row", axis=0, tiled=True),
        preferred_element_type=jnp.float32,
    )
    weight_grad = lax.psum_scatter(
        jnp.einsum("tk,td->kd", whole_attn, grad_out, preferred_element_type=jnp.float32).astype(
            jnp.bfloat16
        ),
        "row",
        scatter_dimension=0,
        tiled=True,
    ).astype(jnp.float32)
    return (branch.astype(jnp.bfloat16), weight_grad)


def solution(mesh):
    in_specs = (
        P("row", None),
        P(),
        P("row", None, "col"),
        P("col", None),
        P("col", None),
        P("col", None, None),
        P("row", "col"),
        P("row", "col"),
    )
    out_specs = (P("row", "col"), P("row", "col"))
    nrow, ncol = mesh.shape["row"], mesh.shape["col"]
    body = per_device
    if (nrow, ncol) == (8, 4):
        body = functools.partial(fast_device, ncol, nrow)
    return jax.shard_map(
        body, mesh=mesh, in_specs=in_specs, out_specs=out_specs, check_vma=False
    )
```

```python
import functools

import jax
import jax.numpy as jnp
from jax import lax
from jax.experimental import pallas as pl
from jax.experimental.pallas import tpu as pltpu
from jax.sharding import PartitionSpec as P

HS = 128
BLOCK = 128
EPS = 1e-06
MESH = pl.DeviceIdType.MESH
SUBS = 2


def norm_rows(values, gain):
    center = jnp.mean(values, axis=-1, keepdims=True)
    shifted = values - center
    variance = jnp.mean(shifted * shifted, axis=-1, keepdims=True)
    return shifted * lax.rsqrt(variance + EPS) * gain


def flip(index, bit):
    return index + bit - 2 * bit * ((index // bit) % 2)


def places():
    row, col = lax.axis_index("row"), lax.axis_index("col")
    return row, col, flip(row, 1), flip(row, 2), flip(row, 4), flip(flip(row, 2), 4)


def remote(src, dst, send, recv, device):
    return pltpu.make_async_remote_copy(
        src_ref=src, dst_ref=dst, send_sem=send, recv_sem=recv, device_id=device, device_id_type=MESH
    )


def project_kernel(ncol, tok_ref, w_ref, qg_ref, kg_ref, out_ref, wbuf, tbuf, acc,
                   w_recv, w_send, t_recv, t_send):
    row, col, mate, xn, yn, dn = places()
    half = (row // 2) % 2
    rows_tok, depth = tbuf.shape[1], tbuf.shape[2]
    per = tbuf.shape[0] // ncol
    tile = w_ref.shape[-1]
    sub = depth // SUBS

    barrier = pltpu.get_barrier_semaphore()
    for other in (mate, xn, yn):
        pl.semaphore_signal(barrier, inc=1, device_id=(other, col), device_id_type=MESH)

    @pl.when(col > 0)
    def _():
        pl.semaphore_signal(barrier, inc=1, device_id=(row, col - 1), device_id_type=MESH)

    @pl.when(col < ncol - 1)
    def _():
        pl.semaphore_signal(barrier, inc=1, device_id=(row, col + 1), device_id_type=MESH)

    pl.semaphore_wait(barrier, 3 + jnp.where(col > 0, 1, 0) + jnp.where(col < ncol - 1, 1, 0))

    def wpart(block, s):
        return wbuf.at[block, :, pl.ds(s * sub, sub)]

    def wown(which, s):
        return w_ref.at[which, :, pl.ds(s * sub, sub)]

    def mine(block):
        return tok_ref.at[:, pl.ds(pl.multiple_of(block * depth, depth), depth)]

    def wcopy(src, block, s, slot, device):
        return remote(src, wpart(block, s), w_send.at[slot, s], w_recv.at[block, s], (device, col))

    def tcopy(src, block, q, slot, device):
        return remote(src, tbuf.at[block], t_send.at[slot, q], t_recv.at[block], device)

    first = [tcopy(mine(col * per + q), col * per + q, q, 0, (xn, col)) for q in range(per)]
    for copy in first:
        copy.start()
    to_y = [wcopy(wown(half, s), row, s, 0, yn) for s in range(SUBS)]
    to_x = [wcopy(wown(1 - half, s), row, s, 1, xn) for s in range(SUBS)]
    to_mate = [wcopy(wown(half, s), row, s, 2, mate) for s in range(SUBS)]
    for copy in to_y + to_mate:
        copy.start()

    own_at = pl.multiple_of(half * rows_tok, rows_tok)
    nbr_at = pl.multiple_of((1 - half) * rows_tok, rows_tok)

    def times(at, left, right, fresh):
        @pl.loop(0, 3)
        def _(t):
            cols = pl.ds(pl.multiple_of(t * tile, tile), tile)
            prod = jnp.dot(left[...], right[t], preferred_element_type=jnp.float32)
            if fresh:
                acc[pl.ds(at, rows_tok), cols] = prod
            else:
                acc[pl.ds(at, rows_tok), cols] += prod

    times(own_at, mine(row), w_ref.at[half], True)

    def up(block, q, slot):
        return tcopy(tbuf.at[block], block, q, slot, (row, col + 1))

    def down(block, q, slot):
        return tcopy(tbuf.at[block], block, q, slot, (row, col - 1))

    def t_got(block):
        tcopy(tbuf.at[block], block, 0, 0, (xn, col)).wait_recv()

    def w_got(block, s):
        wcopy(wpart(block, s), block, s, 0, xn).wait_recv()

    def spread(dist, q):
        if dist == 0:
            block = col * per + q
            t_got(block)

            @pl.when(col < ncol - 1)
            def _():
                up(block, q, 1).start()

            @pl.when(col > 0)
            def _():
                down(block, q, 2).start()
            return

        @pl.when(col >= dist)
        def _():
            block = (col - dist) * per + q
            t_got(block)

            @pl.when(col < ncol - 1)
            def _():
                up(block, q, 2 * dist + 1).start()

        @pl.when(col + dist < ncol)
        def _():
            block = (col + dist) * per + q
            t_got(block)

            @pl.when(col > 0)
            def _():
                down(block, q, 2 * dist + 2).start()

    pend = []

    def pass_w(block, s, slots):
        w_got(block, s)
        for slot, device in slots:
            copy = wcopy(wpart(block, s), block, s, slot, device)
            copy.start()
            pend.append(copy)

    for q in range(per):
        spread(0, q)
    for copy in to_x:
        copy.start()
    pass_w(yn, 0, [(3, mate)])
    spread(1, 0)
    pass_w(yn, 1, [(3, mate)])
    spread(1, 1)
    times(own_at, mine(yn), wbuf.at[yn], False)
    pass_w(xn, 0, [(4, yn), (5, mate)])
    spread(2, 0)
    pass_w(xn, 1, [(4, yn), (5, mate)])
    spread(2, 1)
    times(own_at, mine(xn), wbuf.at[xn], False)
    for block in (mate, flip(mate, 4), flip(mate, 2)):
        for s in range(SUBS):
            w_got(block, s)
        times(own_at, mine(block), wbuf.at[block], False)
    for s in range(SUBS):
        pass_w(dn, s, [(6, mate)])
    times(own_at, mine(dn), wbuf.at[dn], False)
    for dist in range(3, ncol):
        for q in range(per):
            spread(dist, q)
    times(nbr_at, tbuf.at[row], w_ref.at[half], True)
    for block in (mate, flip(mate, 4), flip(mate, 2), yn, xn, dn):
        times(nbr_at, tbuf.at[block], wbuf.at[block], False)
    last = flip(dn, 1)
    for s in range(SUBS):
        w_got(last, s)
    times(own_at, mine(last), wbuf.at[last], False)
    times(nbr_at, tbuf.at[last], wbuf.at[last], False)

    heads = qg_ref.shape[0]
    for kind in range(3):
        for h in range(heads):
            at = (kind * heads + h) * HS
            part = acc[:, at:at + HS]
            if kind < 2:
                part = norm_rows(part, (qg_ref, kg_ref)[kind][h:h + 1, :])
            out_ref[kind, h] = part.astype(jnp.bfloat16)

    for copy in first + to_y + to_x + to_mate + pend:
        copy.wait_send()
    for q in range(per):
        for dist in range(ncol):
            @pl.when((col >= dist) & (col < ncol - 1))
            def _():
                block = (col - dist) * per + q
                up(block, q, 2 * dist + 1).wait_send()

            @pl.when((col + dist < ncol) & (col > 0))
            def _():
                block = (col + dist) * per + q
                down(block, q, 2 * dist + 2).wait_send()


def attend_kernel(ncol, qkv_ref, bias_ref, ow_ref, grad_ref, out_ref, dw_ref,
                  kvbuf, stage, abuf, owbuf, turned, msend, mrecv, dsend, s2, r1, r2,
                  kv_recv, kv_send, ow_recv, ow_send, a_recv, a_send, x_send,
                  m_recv, m_send, r1_recv, r1_send, r2_recv, r2_send):
    row, col, mate, xn, yn, dn = places()
    half = (row // 2) % 2
    heads, rows = qkv_ref.shape[1], qkv_ref.shape[2]
    toks = rows // 2
    here = 2 * (row // 4) + row % 2
    yslot = flip(here, 2)
    barrier = pltpu.get_barrier_semaphore()
    for other in (mate, xn, yn):
        pl.semaphore_signal(barrier, inc=1, device_id=(other, col), device_id_type=MESH)

    @pl.when(col > 0)
    def _():
        pl.semaphore_signal(barrier, inc=1, device_id=(row, col - 1), device_id_type=MESH)

    @pl.when(col < ncol - 1)
    def _():
        pl.semaphore_signal(barrier, inc=1, device_id=(row, col + 1), device_id_type=MESH)

    pl.semaphore_wait(barrier, 3 + jnp.where(col > 0, 1, 0) + jnp.where(col < ncol - 1, 1, 0))
    started = []

    def go(copy):
        copy.start()
        started.append(copy)

    def kv_copy(src, kv, h, slot, way, device):
        return remote(src, kvbuf.at[kv, h, slot], kv_send.at[way, kv, h], kv_recv.at[kv, h, slot], (device, col))

    cut = ow_ref.shape[0] // 2

    def ow_at(block, s):
        return owbuf.at[block, pl.ds(s * cut, cut)]

    def ow_copy(src, block, s, way, device):
        return remote(src, ow_at(block, s), ow_send.at[way, s], ow_recv.at[block, s], (device, col))

    def ow_own(s):
        return ow_ref.at[pl.ds(s * cut, cut)]

    def ow_pass(block, s, ways):
        ow_copy(ow_at(block, s), block, s, 0, xn).wait_recv()
        for way, device in ways:
            go(ow_copy(ow_at(block, s), block, s, way, device))

    for h in range(heads):
        for kv in range(2):
            for way, device in ((0, yn), (1, mate)):
                go(kv_copy(qkv_ref.at[1 + kv, h], kv, h, here, way, device))
            kvbuf[kv, h, here] = qkv_ref[1 + kv, h]
    for s in range(2):
        go(ow_copy(ow_own(s), row, s, 0, xn))
    owbuf[row] = ow_ref[...]
    for h in range(heads):
        for kv in range(2):
            kv_copy(kvbuf.at[kv, h, yslot], kv, h, yslot, 2, mate).wait_recv()
            go(kv_copy(kvbuf.at[kv, h, yslot], kv, h, yslot, 2, mate))
    for s in range(2):
        go(ow_copy(ow_own(s), row, s, 1, yn))
        go(ow_copy(ow_own(s), row, s, 2, mate))

    def a_copy(src, p, way, device):
        return remote(src, abuf.at[p], a_send.at[way, p], a_recv.at[p], device)

    def a_up(p):
        return a_copy(abuf.at[p], p, 0, (row, col + 1))

    def a_down(p):
        return a_copy(abuf.at[p], p, 1, (row, col - 1))

    def a_got(p):
        a_copy(abuf.at[p], p, 0, (xn, col)).wait_recv()

    def piece(plane, other, h):
        side = half + other - 2 * half * other
        return (2 * plane + side) * heads + h

    def z_out(p):
        @pl.when(col < ncol - 1)
        def _():
            a_up(p).start()

        @pl.when(col > 0)
        def _():
            a_down(p).start()

    def x_got(h):
        p = piece(col, 1, h)
        a_got(p)
        z_out(p)

    own_at = pl.ds(pl.multiple_of(half * toks, toks), toks)
    nbr_at = pl.ds(pl.multiple_of((1 - half) * toks, toks), toks)
    scale = HS ** (-0.5)
    for h in range(heads):
        for kv in range(2):
            kv_copy(kvbuf.at[kv, h, 0], kv, h, flip(here, 1), 2, mate).wait_recv()
            kv_copy(kvbuf.at[kv, h, 0], kv, h, flip(yslot, 1), 2, mate).wait_recv()

        @pl.loop(0, rows // BLOCK)
        def _(b):
            at = pl.ds(pl.multiple_of(b * BLOCK, BLOCK), BLOCK)
            keys = kvbuf[0, h].reshape(4 * rows, HS)
            scores = lax.dot_general(qkv_ref[0, h, at, :], keys, (((1,), (1,)), ((), ())),
                                     preferred_element_type=jnp.float32) * scale
            scores = scores + bias_ref[h, b]
            top = jnp.max(scores, axis=-1, keepdims=True)
            expo = jnp.exp(scores - top)
            denom = jnp.sum(expo, axis=-1, keepdims=True)
            prod = jnp.dot(expo.astype(jnp.bfloat16), kvbuf[1, h].reshape(4 * rows, HS),
                           preferred_element_type=jnp.float32)
            stage[h, at, :] = (prod / denom).astype(jnp.bfloat16)

        p = piece(col, 0, h)
        go(remote(stage.at[h, nbr_at], abuf.at[p], x_send.at[h], a_recv.at[p], (xn, col)))
        abuf[p] = stage[h, own_at, :]
        z_out(p)
        if h >= 1:
            x_got(h - 1)
        if h == 0:
            ow_pass(xn, 0, [(3, yn), (4, mate)])
            ow_pass(xn, 1, [(4, mate)])
    x_got(heads - 1)
    ow_pass(yn, 0, [(5, mate)])
    ow_pass(yn, 1, [(3, xn), (5, mate)])
    order = [(0, 0), (0, 1), (1, 0), (0, 2), (1, 1), (1, 2)]
    for dist in range(1, ncol):
        for other, h in order:
            @pl.when(col >= dist)
            def _():
                p = piece(col - dist, other, h)
                a_got(p)

                @pl.when(col < ncol - 1)
                def _():
                    a_up(p).start()

            @pl.when(col + dist < ncol)
            def _():
                p = piece(col + dist, other, h)
                a_got(p)

                @pl.when(col > 0)
                def _():
                    a_down(p).start()
        if dist == 1:
            for s in range(2):
                ow_pass(dn, s, [(6, mate)])

    wide = ow_ref.shape[1]
    tile = wide // 3

    def turn(block):
        turned[...] = jnp.concatenate([abuf[3 * block + i] for i in range(3)], axis=1).T

    def tiles(body):
        @pl.loop(0, 3)
        def _(t):
            body(pl.ds(pl.multiple_of(t * tile, tile), tile))

    def grad_tile(cols):
        return jnp.dot(turned[...], grad_ref[:, cols], preferred_element_type=jnp.float32)

    blocks = (dn, xn, yn, row)

    def m_copy(i):
        return remote(msend.at[i], mrecv.at[i], m_send.at[i], m_recv.at[i], (mate, col))

    for i, block in enumerate(blocks):
        turn(flip(block, 1))

        def to_mate(cols):
            msend[i, :, cols] = grad_tile(cols).astype(jnp.bfloat16)

        tiles(to_mate)
        go(m_copy(i))

    def r1_copy(i, side, through, device):
        return remote(dsend.at[i, pl.ds(side * cut, cut)], r1.at[side, through], r1_send.at[side, through],
                      r1_recv.at[side, through], (device, col))

    def r2_copy(side, device):
        return remote(s2.at[side], r2.at[side], r2_send.at[side], r2_recv.at[side], (device, col))

    for i, block in enumerate(blocks):
        turn(block)
        m_copy(i).wait_recv()

        def total(cols):
            both = grad_tile(cols) + mrecv[i, :, cols].astype(jnp.float32)
            if i < 3:
                dsend[i, :, cols] = both.astype(jnp.bfloat16)
            else:
                dw_ref[:, cols] = both

        tiles(total)
        if i == 0:
            go(r1_copy(0, 0, 1, xn))
            go(r1_copy(0, 1, 1, yn))
        elif i == 1:
            go(r1_copy(1, 0, 0, xn))
        elif i == 2:
            go(r1_copy(2, 1, 0, yn))
    for side, i, source, target in ((1, 1, yn, xn), (0, 2, xn, yn)):
        r1_copy(0, side, 1, source).wait_recv()
        held = dsend[i, side * cut:(side + 1) * cut, :].astype(jnp.float32)
        s2[side] = (held + r1[side, 1].astype(jnp.float32)).astype(jnp.bfloat16)
        go(r2_copy(side, target))

    for block in (mate, flip(xn, 1), flip(yn, 1), flip(dn, 1)):
        for s in range(2):
            ow_copy(ow_at(block, s), block, s, 0, mate).wait_recv()

    def project(cols):
        sums = jnp.zeros((toks, tile), jnp.float32)
        for plane in range(ncol):
            left = jnp.concatenate([abuf[2 * heads * plane + i] for i in range(2 * heads)], axis=1)
            right = owbuf[2 * plane:2 * plane + 2, :, cols].reshape(4 * cut, tile)
            sums += jnp.dot(left, right, preferred_element_type=jnp.float32)
        out_ref[:, cols] = sums.astype(jnp.bfloat16)

    tiles(project)
    for side, near, far in ((0, xn, yn), (1, yn, xn)):
        r1_copy(0, side, 0, near).wait_recv()
        r2_copy(side, far).wait_recv()
        at = slice(side * cut, (side + 1) * cut)
        dw_ref[at, :] += r1[side, 0].astype(jnp.float32) + r2[side].astype(jnp.float32)

    for copy in started:
        copy.wait_send()
    for dist in range(ncol):
        for other, h in order:
            @pl.when((col >= dist) & (col < ncol - 1))
            def _():
                a_up(piece(col - dist, other, h)).wait_send()

            @pl.when((col + dist < ncol) & (col > 0))
            def _():
                a_down(piece(col + dist, other, h)).wait_send()


def vmem(count):
    return [pl.BlockSpec(memory_space=pltpu.VMEM)] * count


def fast_device(ncol, nrow, tokens, ln_gain, qkv_weight, q_gain, k_gain, block_mask, out_weight, grad_out):
    tok_rows, feats = tokens.shape
    depth, _, col_width = qkv_weight.shape
    heads = q_gain.shape[0] // 2
    row = lax.axis_index("row")
    half = (row // 2) % 2
    normed = norm_rows(tokens.astype(jnp.float32), ln_gain).astype(jnp.bfloat16)
    wide = 3 * heads * HS
    by_kind = qkv_weight.transpose(1, 0, 2)
    weight = jnp.stack([by_kind[:, :, :heads * HS], by_kind[:, :, heads * HS:]])
    qg = lax.dynamic_slice_in_dim(q_gain, half * heads, heads, 0)
    kg = lax.dynamic_slice_in_dim(k_gain, half * heads, heads, 0)
    dma = pltpu.SemaphoreType.DMA
    qkv = pl.pallas_call(
        functools.partial(project_kernel, ncol),
        out_shape=jax.ShapeDtypeStruct((3, heads, 2 * tok_rows, HS), jnp.bfloat16),
        in_specs=vmem(4),
        out_specs=vmem(1)[0],
        scratch_shapes=[
            pltpu.VMEM((nrow, 3, depth, heads * HS), jnp.bfloat16),
            pltpu.VMEM((nrow, tok_rows, depth), jnp.bfloat16),
            pltpu.VMEM((2 * tok_rows, wide), jnp.float32),
            dma((nrow, SUBS)), dma((7, SUBS)), dma((nrow,)), dma((2 * ncol + 1, nrow // ncol)),
        ],
        compiler_params=pltpu.CompilerParams(
            collective_id=0, has_side_effects=True, vmem_limit_bytes=56 * 2**20),
        name="project",
    )(normed, weight, qg, kg)

    per = tok_rows // BLOCK
    nblocks = block_mask.shape[1]
    mask = lax.dynamic_slice_in_dim(block_mask, half * heads, heads, 0)
    order = mask.reshape(heads, 2, 2, 2, per, 2, 2, 2, per)
    mine = lax.dynamic_index_in_dim(order, row // 4, 1, False)
    mine = lax.dynamic_index_in_dim(mine, row % 2, 2, False)
    mine = mine.transpose(0, 1, 2, 3, 5, 4, 6).reshape(heads, 2 * per, nblocks)
    bias = jnp.where(mine > 0, 0.0, -1e30).astype(jnp.float32)
    bias = jnp.repeat(bias, BLOCK, axis=2).reshape(heads, 2 * per, 1, nblocks * BLOCK)
    half_rows, out_wide = out_weight.shape[0] // 2, out_weight.shape[1]
    bf = jnp.bfloat16
    return tuple(pl.pallas_call(
        functools.partial(attend_kernel, ncol),
        out_shape=[jax.ShapeDtypeStruct((tok_rows, out_wide), bf),
                   jax.ShapeDtypeStruct(out_weight.shape, jnp.float32)],
        in_specs=vmem(4),
        out_specs=vmem(2),
        scratch_shapes=[
            pltpu.VMEM((2, heads, 4, 2 * tok_rows, HS), bf),
            pltpu.VMEM((heads, 2 * tok_rows, HS), bf),
            pltpu.VMEM((2 * ncol * heads, tok_rows, HS), bf),
            pltpu.VMEM((nrow, *out_weight.shape), bf),
            pltpu.VMEM((heads * HS, tok_rows), bf),
            pltpu.VMEM((4, *out_weight.shape), bf),
            pltpu.VMEM((4, *out_weight.shape), bf),
            pltpu.VMEM((3, *out_weight.shape), bf),
            pltpu.VMEM((2, half_rows, out_wide), bf),
            pltpu.VMEM((2, 2, half_rows, out_wide), bf),
            pltpu.VMEM((2, half_rows, out_wide), bf),
            dma((2, heads, 4)), dma((3, 2, heads)), dma((nrow, 2)), dma((7, 2)),
            dma((2 * ncol * heads,)), dma((2, 2 * ncol * heads)), dma((heads,)),
            dma((4,)), dma((4,)), dma((2, 2)), dma((2, 2)), dma((2,)), dma((2,)),
        ],
        compiler_params=pltpu.CompilerParams(
            collective_id=1, has_side_effects=True, vmem_limit_bytes=60 * 2**20),
        name="attend",
    )(qkv, bias, out_weight, grad_out))


def per_device(tokens, ln_gain, qkv_weight, q_gain, k_gain, block_mask, out_weight, grad_out):
    tok_rows = tokens.shape[0]
    heads_here = q_gain.shape[0]
    col_width = heads_here * HS
    normed = norm_rows(tokens.astype(jnp.float32), ln_gain).astype(jnp.bfloat16)
    portion = lax.all_gather(qkv_weight, "row", axis=0, tiled=True)
    flat_part = portion.reshape(portion.shape[0], 3 * col_width)
    mixed = jnp.dot(normed, flat_part, preferred_element_type=jnp.float32)
    mixed = mixed.reshape(tok_rows, 3, heads_here, HS)
    queries = norm_rows(mixed[:, 0], q_gain).astype(jnp.bfloat16)
    keys_here = norm_rows(mixed[:, 1], k_gain).astype(jnp.bfloat16)
    values_here = mixed[:, 2].astype(jnp.bfloat16)
    nblocks = block_mask.shape[1]
    qblocks = tok_rows // BLOCK
    first_block = lax.axis_index("row") * qblocks
    mask_rows = lax.dynamic_slice_in_dim(block_mask, first_block, qblocks, 1)
    query_blocks = queries.reshape(qblocks, BLOCK, heads_here, HS)
    key_part = lax.all_gather(keys_here, "row", axis=0, tiled=True)
    value_part = lax.all_gather(values_here, "row", axis=0, tiled=True)
    scores = (
        jnp.einsum("abhd,khd->habk", query_blocks, key_part, preferred_element_type=jnp.float32)
        * HS ** (-0.5)
    )
    is_live = jnp.repeat(mask_rows > 0, BLOCK, axis=2)[:, :, None, :]
    scores = jnp.where(is_live, scores, -1e30)
    top = jnp.max(scores, axis=-1, keepdims=True)
    expo = jnp.where(is_live, jnp.exp(scores - top), 0.0)
    denom = jnp.sum(expo, axis=-1)
    accum = jnp.einsum(
        "habk,khd->habd", expo.astype(jnp.bfloat16), value_part, preferred_element_type=jnp.float32
    )
    attn_here = (accum / denom[..., None]).astype(jnp.bfloat16)
    attn_here = attn_here.transpose(1, 2, 0, 3).reshape(tok_rows, col_width)
    whole_attn = lax.all_gather(attn_here, "col", axis=1, tiled=True)
    branch = jnp.dot(
        whole_attn,
        lax.all_gather(out_weight, "row", axis=0, tiled=True),
        preferred_element_type=jnp.float32,
    )
    weight_grad = lax.psum_scatter(
        jnp.einsum("tk,td->kd", whole_attn, grad_out, preferred_element_type=jnp.float32).astype(
            jnp.bfloat16
        ),
        "row",
        scatter_dimension=0,
        tiled=True,
    ).astype(jnp.float32)
    return (branch.astype(jnp.bfloat16), weight_grad)


def solution(mesh):
    in_specs = (
        P("row", None),
        P(),
        P("row", None, "col"),
        P("col", None),
        P("col", None),
        P("col", None, None),
        P("row", "col"),
        P("row", "col"),
    )
    out_specs = (P("row", "col"), P("row", "col"))
    nrow, ncol = mesh.shape["row"], mesh.shape["col"]
    body = per_device
    if (nrow, ncol) == (8, 4):
        body = functools.partial(fast_device, ncol, nrow)
    return jax.shard_map(
        body, mesh=mesh, in_specs=in_specs, out_specs=out_specs, check_vma=False
    )
```

```python
import functools

import jax
import jax.numpy as jnp
from jax import lax
from jax.experimental import pallas as pl
from jax.experimental.pallas import tpu as pltpu
from jax.sharding import PartitionSpec as P

HS = 128
BLOCK = 128
EPS = 1e-06
MESH = pl.DeviceIdType.MESH
SUBS = 2


def norm_rows(values, gain):
    center = jnp.mean(values, axis=-1, keepdims=True)
    shifted = values - center
    variance = jnp.mean(shifted * shifted, axis=-1, keepdims=True)
    return shifted * lax.rsqrt(variance + EPS) * gain


def flip(index, bit):
    return index + bit - 2 * bit * ((index // bit) % 2)


def places():
    row, col = lax.axis_index("row"), lax.axis_index("col")
    return row, col, flip(row, 1), flip(row, 2), flip(row, 4), flip(flip(row, 2), 4)


def remote(src, dst, send, recv, device):
    return pltpu.make_async_remote_copy(
        src_ref=src, dst_ref=dst, send_sem=send, recv_sem=recv, device_id=device, device_id_type=MESH
    )


def project_kernel(ncol, tok_ref, w_ref, qg_ref, kg_ref, out_ref, wbuf, tbuf, acc,
                   w_recv, w_send, t_recv, t_send):
    row, col, mate, xn, yn, dn = places()
    half = (row // 2) % 2
    rows_tok, depth = tbuf.shape[1], tbuf.shape[2]
    per = tbuf.shape[0] // ncol
    tile = wbuf.shape[-1]
    sub = depth // SUBS

    barrier = pltpu.get_barrier_semaphore()
    for other in (mate, xn, yn):
        pl.semaphore_signal(barrier, inc=1, device_id=(other, col), device_id_type=MESH)

    @pl.when(col > 0)
    def _():
        pl.semaphore_signal(barrier, inc=1, device_id=(row, col - 1), device_id_type=MESH)

    @pl.when(col < ncol - 1)
    def _():
        pl.semaphore_signal(barrier, inc=1, device_id=(row, col + 1), device_id_type=MESH)

    pl.semaphore_wait(barrier, 3 + jnp.where(col > 0, 1, 0) + jnp.where(col < ncol - 1, 1, 0))

    def wpart(block, s):
        return wbuf.at[block, :, pl.ds(s * sub, sub)]

    def wown(which, s):
        return w_ref.at[:, pl.ds(s * sub, sub), pl.ds(pl.multiple_of(which * tile, tile), tile)]

    def mine(block):
        return tok_ref.at[:, pl.ds(pl.multiple_of(block * depth, depth), depth)]

    def wcopy(src, block, s, slot, device):
        return remote(src, wpart(block, s), w_send.at[slot, s], w_recv.at[block, s], (device, col))

    def tcopy(src, block, q, slot, device):
        return remote(src, tbuf.at[block], t_send.at[slot, q], t_recv.at[block], device)

    first = [tcopy(mine(col * per + q), col * per + q, q, 0, (xn, col)) for q in range(per)]
    for copy in first:
        copy.start()
    to_y = [wcopy(wown(half, s), row, s, 0, yn) for s in range(SUBS)]
    to_x = [wcopy(wown(1 - half, s), row, s, 1, xn) for s in range(SUBS)]
    to_mate = [wcopy(wown(half, s), row, s, 2, mate) for s in range(SUBS)]
    for copy in to_y + to_mate:
        copy.start()

    own_at = pl.multiple_of(half * rows_tok, rows_tok)
    nbr_at = pl.multiple_of((1 - half) * rows_tok, rows_tok)

    def times(at, left, right, fresh):
        @pl.loop(0, 3)
        def _(t):
            cols = pl.ds(pl.multiple_of(t * tile, tile), tile)
            prod = jnp.dot(left[...], right[t], preferred_element_type=jnp.float32)
            if fresh:
                acc[pl.ds(at, rows_tok), cols] = prod
            else:
                acc[pl.ds(at, rows_tok), cols] += prod

    wbuf[row] = w_ref[:, :, pl.ds(pl.multiple_of(half * tile, tile), tile)]
    acc[pl.ds(nbr_at, rows_tok)] = jnp.zeros((rows_tok, acc.shape[1]), jnp.float32)
    times(own_at, mine(row), wbuf.at[row], True)

    def up(block, q, slot):
        return tcopy(tbuf.at[block], block, q, slot, (row, col + 1))

    def down(block, q, slot):
        return tcopy(tbuf.at[block], block, q, slot, (row, col - 1))

    def t_got(block):
        tcopy(tbuf.at[block], block, 0, 0, (xn, col)).wait_recv()

    def w_got(block, s):
        wcopy(wpart(block, s), block, s, 0, xn).wait_recv()

    def spread(dist, q):
        if dist == 0:
            block = col * per + q
            t_got(block)

            @pl.when(col < ncol - 1)
            def _():
                up(block, q, 1).start()

            @pl.when(col > 0)
            def _():
                down(block, q, 2).start()
            return

        @pl.when(col >= dist)
        def _():
            block = (col - dist) * per + q
            t_got(block)

            @pl.when(col < ncol - 1)
            def _():
                up(block, q, 2 * dist + 1).start()

        @pl.when(col + dist < ncol)
        def _():
            block = (col + dist) * per + q
            t_got(block)

            @pl.when(col > 0)
            def _():
                down(block, q, 2 * dist + 2).start()

    pend = []

    def pass_w(block, s, slots):
        w_got(block, s)
        for slot, device in slots:
            copy = wcopy(wpart(block, s), block, s, slot, device)
            copy.start()
            pend.append(copy)

    for q in range(per):
        spread(0, q)
    for copy in to_x:
        copy.start()
    pass_w(yn, 0, [(3, mate)])
    spread(1, 0)
    pass_w(yn, 1, [(3, mate)])
    spread(1, 1)
    times(own_at, mine(yn), wbuf.at[yn], False)
    pass_w(xn, 0, [(4, yn), (5, mate)])
    spread(2, 0)
    pass_w(xn, 1, [(4, yn), (5, mate)])
    spread(2, 1)
    times(own_at, mine(xn), wbuf.at[xn], False)
    for block in (mate, flip(mate, 4), flip(mate, 2)):
        for s in range(SUBS):
            w_got(block, s)
        times(own_at, mine(block), wbuf.at[block], False)
    def early(q):
        return (q != dn // 2) & (q - col <= 2) & (col - q <= 2)

    def quarter(q):
        for i in range(per):
            times(nbr_at, tbuf.at[per * q + i], wbuf.at[per * q + i], False)

    @pl.loop(0, ncol)
    def _(q):
        @pl.when(early(q))
        def _():
            quarter(q)

    for s in range(SUBS):
        pass_w(dn, s, [(6, mate)])
    times(own_at, mine(dn), wbuf.at[dn], False)
    for dist in range(3, ncol):
        for q in range(per):
            spread(dist, q)
    last = flip(dn, 1)
    for s in range(SUBS):
        w_got(last, s)
    times(own_at, mine(last), wbuf.at[last], False)

    @pl.loop(0, ncol)
    def _(q):
        @pl.when(jnp.logical_not(early(q)))
        def _():
            quarter(q)

    heads = qg_ref.shape[0]
    for kind in range(3):
        for h in range(heads):
            at = (kind * heads + h) * HS
            part = acc[:, at:at + HS]
            if kind < 2:
                part = norm_rows(part, (qg_ref, kg_ref)[kind][h:h + 1, :])
            out_ref[kind, h] = part.astype(jnp.bfloat16)

    for copy in first + to_y + to_x + to_mate + pend:
        copy.wait_send()
    for q in range(per):
        for dist in range(ncol):
            @pl.when((col >= dist) & (col < ncol - 1))
            def _():
                block = (col - dist) * per + q
                up(block, q, 2 * dist + 1).wait_send()

            @pl.when((col + dist < ncol) & (col > 0))
            def _():
                block = (col + dist) * per + q
                down(block, q, 2 * dist + 2).wait_send()


def attend_kernel(ncol, qkv_ref, bias_ref, ow_ref, grad_ref, out_ref, dw_ref,
                  kvbuf, stage, abuf, owbuf, turned, msend, mrecv, dsend, s2, r1, r2,
                  kv_recv, kv_send, ow_recv, ow_send, a_recv, a_send, x_send,
                  m_recv, m_send, r1_recv, r1_send, r2_recv, r2_send):
    row, col, mate, xn, yn, dn = places()
    half = (row // 2) % 2
    heads, rows = qkv_ref.shape[1], qkv_ref.shape[2]
    toks = rows // 2
    here = 2 * (row // 4) + row % 2
    yslot = flip(here, 2)
    barrier = pltpu.get_barrier_semaphore()
    for other in (mate, xn, yn):
        pl.semaphore_signal(barrier, inc=1, device_id=(other, col), device_id_type=MESH)

    @pl.when(col > 0)
    def _():
        pl.semaphore_signal(barrier, inc=1, device_id=(row, col - 1), device_id_type=MESH)

    @pl.when(col < ncol - 1)
    def _():
        pl.semaphore_signal(barrier, inc=1, device_id=(row, col + 1), device_id_type=MESH)

    pl.semaphore_wait(barrier, 3 + jnp.where(col > 0, 1, 0) + jnp.where(col < ncol - 1, 1, 0))
    started = []

    def go(copy):
        copy.start()
        started.append(copy)

    def kv_copy(src, kv, h, slot, way, device):
        return remote(src, kvbuf.at[kv, h, slot], kv_send.at[way, kv, h], kv_recv.at[kv, h, slot], (device, col))

    cut = ow_ref.shape[0] // 2

    def ow_at(block, s):
        return owbuf.at[block, pl.ds(s * cut, cut)]

    def ow_copy(src, block, s, way, device):
        return remote(src, ow_at(block, s), ow_send.at[way, s], ow_recv.at[block, s], (device, col))

    def ow_own(s):
        return ow_ref.at[pl.ds(s * cut, cut)]

    def ow_pass(block, s, ways):
        ow_copy(ow_at(block, s), block, s, 0, xn).wait_recv()
        for way, device in ways:
            go(ow_copy(ow_at(block, s), block, s, way, device))

    for h in range(heads):
        for kv in range(2):
            for way, device in ((0, yn), (1, mate)):
                go(kv_copy(qkv_ref.at[1 + kv, h], kv, h, here, way, device))
            kvbuf[kv, h, here] = qkv_ref[1 + kv, h]
    for s in range(2):
        go(ow_copy(ow_own(s), row, s, 0, xn))
    owbuf[row] = ow_ref[...]
    for h in range(heads):
        for kv in range(2):
            kv_copy(kvbuf.at[kv, h, yslot], kv, h, yslot, 2, mate).wait_recv()
            go(kv_copy(kvbuf.at[kv, h, yslot], kv, h, yslot, 2, mate))
    for s in range(2):
        go(ow_copy(ow_own(s), row, s, 1, yn))
        go(ow_copy(ow_own(s), row, s, 2, mate))

    def a_copy(src, p, way, device):
        return remote(src, abuf.at[p], a_send.at[way, p], a_recv.at[p], device)

    def a_up(p):
        return a_copy(abuf.at[p], p, 0, (row, col + 1))

    def a_down(p):
        return a_copy(abuf.at[p], p, 1, (row, col - 1))

    def a_got(p):
        a_copy(abuf.at[p], p, 0, (xn, col)).wait_recv()

    def piece(plane, other, h):
        side = half + other - 2 * half * other
        return (2 * plane + side) * heads + h

    def z_out(p):
        @pl.when(col < ncol - 1)
        def _():
            a_up(p).start()

        @pl.when(col > 0)
        def _():
            a_down(p).start()

    def x_got(h):
        p = piece(col, 1, h)
        a_got(p)
        z_out(p)

    own_at = pl.ds(pl.multiple_of(half * toks, toks), toks)
    nbr_at = pl.ds(pl.multiple_of((1 - half) * toks, toks), toks)
    scale = HS ** (-0.5)
    for h in range(heads):
        for kv in range(2):
            kv_copy(kvbuf.at[kv, h, 0], kv, h, flip(here, 1), 2, mate).wait_recv()
            kv_copy(kvbuf.at[kv, h, 0], kv, h, flip(yslot, 1), 2, mate).wait_recv()

        @pl.loop(0, rows // BLOCK)
        def _(b):
            at = pl.ds(pl.multiple_of(b * BLOCK, BLOCK), BLOCK)
            keys = kvbuf[0, h].reshape(4 * rows, HS)
            scores = lax.dot_general(qkv_ref[0, h, at, :], keys, (((1,), (1,)), ((), ())),
                                     preferred_element_type=jnp.float32) * scale
            scores = scores + bias_ref[h, b]
            top = jnp.max(scores, axis=-1, keepdims=True)
            expo = jnp.exp(scores - top)
            denom = jnp.sum(expo, axis=-1, keepdims=True)
            prod = jnp.dot(expo.astype(jnp.bfloat16), kvbuf[1, h].reshape(4 * rows, HS),
                           preferred_element_type=jnp.float32)
            stage[h, at, :] = (prod / denom).astype(jnp.bfloat16)

        p = piece(col, 0, h)
        go(remote(stage.at[h, nbr_at], abuf.at[p], x_send.at[h], a_recv.at[p], (xn, col)))
        abuf[p] = stage[h, own_at, :]
        z_out(p)
        if h >= 1:
            x_got(h - 1)
        if h == 0:
            ow_pass(xn, 0, [(3, yn), (4, mate)])
            ow_pass(xn, 1, [(4, mate)])
    x_got(heads - 1)
    ow_pass(yn, 0, [(5, mate)])
    ow_pass(yn, 1, [(3, xn), (5, mate)])
    wide = ow_ref.shape[1]
    tile = wide // 3

    def turn(block):
        turned[...] = jnp.concatenate([abuf[3 * block + i] for i in range(3)], axis=1).T

    def tiles(body):
        @pl.loop(0, 3)
        def _(t):
            body(pl.ds(pl.multiple_of(t * tile, tile), tile))

    def grad_tile(cols):
        return jnp.dot(turned[...], grad_ref[:, cols], preferred_element_type=jnp.float32)

    def m_copy(i):
        return remote(msend.at[i], mrecv.at[i], m_send.at[i], m_recv.at[i], (mate, col))

    def mate_block(plane):
        chip = row // 2
        code = 2 * ((plane // 2 + chip // 2) % 2) + (plane + chip) % 2
        i = jnp.where(code == 0, 3, jnp.where(code == 3, 0, code))
        turn(2 * plane + 1 - row % 2)

        def to_mate(cols):
            msend[i, :, cols] = grad_tile(cols).astype(jnp.bfloat16)

        tiles(to_mate)
        m_copy(i).start()

    order = [(0, 0), (0, 1), (1, 0), (0, 2), (1, 1), (1, 2)]
    mate_block(col)
    for dist in range(1, ncol):
        for other, h in order:
            @pl.when(col >= dist)
            def _():
                p = piece(col - dist, other, h)
                a_got(p)

                @pl.when(col < ncol - 1)
                def _():
                    a_up(p).start()

            @pl.when(col + dist < ncol)
            def _():
                p = piece(col + dist, other, h)
                a_got(p)

                @pl.when(col > 0)
                def _():
                    a_down(p).start()
        @pl.when(col >= dist)
        def _():
            mate_block(col - dist)

        @pl.when(col + dist < ncol)
        def _():
            mate_block(col + dist)

        if dist == 1:
            for s in range(2):
                ow_pass(dn, s, [(6, mate)])

    blocks = (dn, xn, yn, row)

    def r1_copy(i, side, through, device):
        return remote(dsend.at[i, pl.ds(side * cut, cut)], r1.at[side, through], r1_send.at[side, through],
                      r1_recv.at[side, through], (device, col))

    def r2_copy(side, device):
        return remote(s2.at[side], r2.at[side], r2_send.at[side], r2_recv.at[side], (device, col))

    for i, block in enumerate(blocks):
        turn(block)
        m_copy(i).wait_recv()

        def total(cols):
            both = grad_tile(cols) + mrecv[i, :, cols].astype(jnp.float32)
            if i < 3:
                dsend[i, :, cols] = both.astype(jnp.bfloat16)
            else:
                dw_ref[:, cols] = both

        tiles(total)
        if i == 0:
            go(r1_copy(0, 0, 1, xn))
            go(r1_copy(0, 1, 1, yn))
        elif i == 1:
            go(r1_copy(1, 0, 0, xn))
        elif i == 2:
            go(r1_copy(2, 1, 0, yn))
    for side, i, source, target in ((1, 1, yn, xn), (0, 2, xn, yn)):
        r1_copy(0, side, 1, source).wait_recv()
        held = dsend[i, side * cut:(side + 1) * cut, :].astype(jnp.float32)
        s2[side] = (held + r1[side, 1].astype(jnp.float32)).astype(jnp.bfloat16)
        go(r2_copy(side, target))

    for block in (mate, flip(xn, 1), flip(yn, 1), flip(dn, 1)):
        for s in range(2):
            ow_copy(ow_at(block, s), block, s, 0, mate).wait_recv()

    def project(cols):
        sums = jnp.zeros((toks, tile), jnp.float32)
        for plane in range(ncol):
            left = jnp.concatenate([abuf[2 * heads * plane + i] for i in range(2 * heads)], axis=1)
            right = owbuf[2 * plane:2 * plane + 2, :, cols].reshape(4 * cut, tile)
            sums += jnp.dot(left, right, preferred_element_type=jnp.float32)
        out_ref[:, cols] = sums.astype(jnp.bfloat16)

    tiles(project)
    for side, near, far in ((0, xn, yn), (1, yn, xn)):
        r1_copy(0, side, 0, near).wait_recv()
        r2_copy(side, far).wait_recv()
        at = slice(side * cut, (side + 1) * cut)
        dw_ref[at, :] += r1[side, 0].astype(jnp.float32) + r2[side].astype(jnp.float32)

    for copy in started:
        copy.wait_send()
    for i in range(4):
        m_copy(i).wait_send()
    for dist in range(ncol):
        for other, h in order:
            @pl.when((col >= dist) & (col < ncol - 1))
            def _():
                a_up(piece(col - dist, other, h)).wait_send()

            @pl.when((col + dist < ncol) & (col > 0))
            def _():
                a_down(piece(col + dist, other, h)).wait_send()


def vmem(count):
    return [pl.BlockSpec(memory_space=pltpu.VMEM)] * count


def fast_device(ncol, nrow, tokens, ln_gain, qkv_weight, q_gain, k_gain, block_mask, out_weight, grad_out):
    tok_rows, feats = tokens.shape
    depth, _, col_width = qkv_weight.shape
    heads = q_gain.shape[0] // 2
    row = lax.axis_index("row")
    half = (row // 2) % 2
    normed = norm_rows(tokens.astype(jnp.float32), ln_gain).astype(jnp.bfloat16)
    wide = 3 * heads * HS
    weight = qkv_weight.transpose(1, 0, 2)
    qg = lax.dynamic_slice_in_dim(q_gain, half * heads, heads, 0)
    kg = lax.dynamic_slice_in_dim(k_gain, half * heads, heads, 0)
    dma = pltpu.SemaphoreType.DMA
    qkv = pl.pallas_call(
        functools.partial(project_kernel, ncol),
        out_shape=jax.ShapeDtypeStruct((3, heads, 2 * tok_rows, HS), jnp.bfloat16),
        in_specs=vmem(4),
        out_specs=vmem(1)[0],
        scratch_shapes=[
            pltpu.VMEM((nrow, 3, depth, heads * HS), jnp.bfloat16),
            pltpu.VMEM((nrow, tok_rows, depth), jnp.bfloat16),
            pltpu.VMEM((2 * tok_rows, wide), jnp.float32),
            dma((nrow, SUBS)), dma((7, SUBS)), dma((nrow,)), dma((2 * ncol + 1, nrow // ncol)),
        ],
        compiler_params=pltpu.CompilerParams(
            collective_id=0, has_side_effects=True, vmem_limit_bytes=56 * 2**20),
        name="project",
    )(normed, weight, qg, kg)

    per = tok_rows // BLOCK
    nblocks = block_mask.shape[1]
    mask = lax.dynamic_slice_in_dim(block_mask, half * heads, heads, 0)
    order = mask.reshape(heads, 2, 2, 2, per, 2, 2, 2, per)
    mine = lax.dynamic_index_in_dim(order, row // 4, 1, False)
    mine = lax.dynamic_index_in_dim(mine, row % 2, 2, False)
    mine = mine.transpose(0, 1, 2, 3, 5, 4, 6).reshape(heads, 2 * per, nblocks)
    bias = jnp.where(mine > 0, 0.0, -1e30).astype(jnp.float32)
    bias = jnp.repeat(bias, BLOCK, axis=2).reshape(heads, 2 * per, 1, nblocks * BLOCK)
    half_rows, out_wide = out_weight.shape[0] // 2, out_weight.shape[1]
    bf = jnp.bfloat16
    return tuple(pl.pallas_call(
        functools.partial(attend_kernel, ncol),
        out_shape=[jax.ShapeDtypeStruct((tok_rows, out_wide), bf),
                   jax.ShapeDtypeStruct(out_weight.shape, jnp.float32)],
        in_specs=vmem(4),
        out_specs=vmem(2),
        scratch_shapes=[
            pltpu.VMEM((2, heads, 4, 2 * tok_rows, HS), bf),
            pltpu.VMEM((heads, 2 * tok_rows, HS), bf),
            pltpu.VMEM((2 * ncol * heads, tok_rows, HS), bf),
            pltpu.VMEM((nrow, *out_weight.shape), bf),
            pltpu.VMEM((heads * HS, tok_rows), bf),
            pltpu.VMEM((4, *out_weight.shape), bf),
            pltpu.VMEM((4, *out_weight.shape), bf),
            pltpu.VMEM((3, *out_weight.shape), bf),
            pltpu.VMEM((2, half_rows, out_wide), bf),
            pltpu.VMEM((2, 2, half_rows, out_wide), bf),
            pltpu.VMEM((2, half_rows, out_wide), bf),
            dma((2, heads, 4)), dma((3, 2, heads)), dma((nrow, 2)), dma((7, 2)),
            dma((2 * ncol * heads,)), dma((2, 2 * ncol * heads)), dma((heads,)),
            dma((4,)), dma((4,)), dma((2, 2)), dma((2, 2)), dma((2,)), dma((2,)),
        ],
        compiler_params=pltpu.CompilerParams(
            collective_id=1, has_side_effects=True, vmem_limit_bytes=60 * 2**20),
        name="attend",
    )(qkv, bias, out_weight, grad_out))


def per_device(tokens, ln_gain, qkv_weight, q_gain, k_gain, block_mask, out_weight, grad_out):
    tok_rows = tokens.shape[0]
    heads_here = q_gain.shape[0]
    col_width = heads_here * HS
    normed = norm_rows(tokens.astype(jnp.float32), ln_gain).astype(jnp.bfloat16)
    portion = lax.all_gather(qkv_weight, "row", axis=0, tiled=True)
    flat_part = portion.reshape(portion.shape[0], 3 * col_width)
    mixed = jnp.dot(normed, flat_part, preferred_element_type=jnp.float32)
    mixed = mixed.reshape(tok_rows, 3, heads_here, HS)
    queries = norm_rows(mixed[:, 0], q_gain).astype(jnp.bfloat16)
    keys_here = norm_rows(mixed[:, 1], k_gain).astype(jnp.bfloat16)
    values_here = mixed[:, 2].astype(jnp.bfloat16)
    nblocks = block_mask.shape[1]
    qblocks = tok_rows // BLOCK
    first_block = lax.axis_index("row") * qblocks
    mask_rows = lax.dynamic_slice_in_dim(block_mask, first_block, qblocks, 1)
    query_blocks = queries.reshape(qblocks, BLOCK, heads_here, HS)
    key_part = lax.all_gather(keys_here, "row", axis=0, tiled=True)
    value_part = lax.all_gather(values_here, "row", axis=0, tiled=True)
    scores = (
        jnp.einsum("abhd,khd->habk", query_blocks, key_part, preferred_element_type=jnp.float32)
        * HS ** (-0.5)
    )
    is_live = jnp.repeat(mask_rows > 0, BLOCK, axis=2)[:, :, None, :]
    scores = jnp.where(is_live, scores, -1e30)
    top = jnp.max(scores, axis=-1, keepdims=True)
    expo = jnp.where(is_live, jnp.exp(scores - top), 0.0)
    denom = jnp.sum(expo, axis=-1)
    accum = jnp.einsum(
        "habk,khd->habd", expo.astype(jnp.bfloat16), value_part, preferred_element_type=jnp.float32
    )
    attn_here = (accum / denom[..., None]).astype(jnp.bfloat16)
    attn_here = attn_here.transpose(1, 2, 0, 3).reshape(tok_rows, col_width)
    whole_attn = lax.all_gather(attn_here, "col", axis=1, tiled=True)
    branch = jnp.dot(
        whole_attn,
        lax.all_gather(out_weight, "row", axis=0, tiled=True),
        preferred_element_type=jnp.float32,
    )
    weight_grad = lax.psum_scatter(
        jnp.einsum("tk,td->kd", whole_attn, grad_out, preferred_element_type=jnp.float32).astype(
            jnp.bfloat16
        ),
        "row",
        scatter_dimension=0,
        tiled=True,
    ).astype(jnp.float32)
    return (branch.astype(jnp.bfloat16), weight_grad)


def solution(mesh):
    in_specs = (
        P("row", None),
        P(),
        P("row", None, "col"),
        P("col", None),
        P("col", None),
        P("col", None, None),
        P("row", "col"),
        P("row", "col"),
    )
    out_specs = (P("row", "col"), P("row", "col"))
    nrow, ncol = mesh.shape["row"], mesh.shape["col"]
    body = per_device
    if (nrow, ncol) == (8, 4):
        body = functools.partial(fast_device, ncol, nrow)
    return jax.shard_map(
        body, mesh=mesh, in_specs=in_specs, out_specs=out_specs, check_vma=False
    )
```
